32 devices in a mesh: wide: 16 (over z, y, x), narrow: 2 (over core).
Axes of the slice: x: 2, y: 2, z: 4, core: 2. Of those that a mesh axis runs over, the one named last changes fastest.
Arguments:
- plan_logits: float32 [2, 2, 2, 32, 1024], P(None, 'narrow'), may hold values from 0 to 3
- pot_size: float32 [2, 2], P('narrow'), may hold values from 0.5 to 2
- payoff_tiles: bfloat16 [32, 1024, 1024], P(('wide', 'narrow')), may hold values from -0.046875 to 0.046875
- parent_first: int32 [32], P(('wide', 'narrow')), may hold values from 0 to 1
- parent_second: int32 [32], P(('wide', 'narrow')), may hold values from 0 to 1
Outputs:
- new_logits: float32 [2, 2, 2, 32, 1024], P(None, 'narrow')
- line_utility: float32 [2, 2, 32, 1024], replicated
The draws below stay inside these ranges and needn't reach their ends.
All inputs are finite; a program needn't handle non-finite values.
Results may differ from the reference program's by a relative error of at most 0.0031.
Values may be sent and summed in bfloat16 or wider, within the bound.
A program may use at most 64 MiB of HBM per device.

```python
import jax
import jax.numpy as jnp
from jax import lax

B = 1024
BELIEFS = 32
LINES = 2
STEPS = 3
LEVELS = 2
LEAVES = 32


def touch_ends(drawn, rng, least, largest):
    index_at = [jax.random.randint(jax.random.fold_in(rng, axis), (), 0, length) for axis, length in enumerate(drawn.shape)]
    main_axis = drawn.shape.index(max(drawn.shape))
    beside = index_at[:main_axis] + [(index_at[main_axis] + 1) % drawn.shape[main_axis]] + index_at[main_axis + 1:]
    return drawn.at[tuple(index_at)].set(least).at[tuple(beside)].set(largest)


def block_scale(own_key, dims, cuts, smallest, high):
    def one(dim, shards_of):
        heights = jax.random.uniform(jax.random.fold_in(jax.random.fold_in(own_key, 6), dim), (shards_of,), jnp.float32, smallest / len(cuts), high / len(cuts))
        return jnp.repeat(jnp.exp(heights), dims[dim] // shards_of).reshape((-1,) + (1,) * (len(dims) - dim - 1))

    factor_of = one(*cuts[0])
    for cut in cuts[1:]:
        factor_of = factor_of * one(*cut)
    return factor_of


def gaussian(own_key, extent, spread, bound, shards=(), held_as=jnp.bfloat16):
    drawn = spread * jax.random.normal(own_key, extent, jnp.float32)
    if shards:
        drawn = drawn * block_scale(own_key, extent, shards, -0.22, 0.18)
    return jnp.clip(drawn, -bound, bound).astype(held_as)


def setup_inputs(seed: int = 0) -> dict:
    streams_of = jax.random.split(jax.random.key(seed), 6)
    return {
        "plan_logits": jnp.clip(3.0 * jax.random.uniform(streams_of[0], (2, LEVELS, LINES, BELIEFS, B), jnp.float32) ** block_scale(streams_of[0], (2, LEVELS, LINES, BELIEFS, B), ((1, 2),), -0.2, 0.2), 0.0, 3.0),
        "pot_size": jnp.clip(0.5 + 1.5 * jax.random.uniform(streams_of[1], (LEVELS, LINES), jnp.float32) ** block_scale(streams_of[1], (LEVELS, LINES), ((0, 2),), -0.2, 0.2), 0.5, 2.0),
        "payoff_tiles": gaussian(streams_of[2], (LEAVES, B, B), (B * LEAVES // LINES) ** -0.5, 0.046875, ((0, 32),)),
        "parent_first": touch_ends(jax.random.randint(streams_of[3], (LEAVES,), 0, LINES), jax.random.fold_in(streams_of[3], 1), 0, LINES - 1).astype(jnp.int32),
        "parent_second": touch_ends(jax.random.randint(streams_of[4], (LEAVES,), 0, LINES), jax.random.fold_in(streams_of[4], 1), 0, LINES - 1).astype(jnp.int32),
    }


learning_rate = 1.0


def reference(plan_logits, pot_size, payoff_tiles, parent_first, parent_second):
    logits = plan_logits
    previous = None
    utility = None
    for iteration in range(STEPS):
        keep = jax.nn.log_sigmoid(logits)
        prefix = jnp.cumsum(keep, axis=1) - keep
        full_reach = jnp.exp(jnp.sum(keep, axis=1)).astype(jnp.bfloat16)

        def leaf_step(carry, items):
            tile, first_line, second_line = items
            first_reach = full_reach[0, first_line]
            second_reach = full_reach[1, second_line]
            value_first = jnp.dot(second_reach, tile.T, preferred_element_type=jnp.float32)
            value_second = -jnp.dot(first_reach, tile, preferred_element_type=jnp.float32)
            carry = carry.at[0, first_line].add(value_first)
            carry = carry.at[1, second_line].add(value_second)
            return carry, None

        start = jnp.zeros((2, LINES, BELIEFS, B), jnp.float32)
        utility, _ = lax.scan(leaf_step, start, (payoff_tiles, parent_first, parent_second))
        if previous is None:
            previous = utility
        target = 2.0 * utility - previous
        previous = utility
        opp_mass = jnp.mean(jnp.exp(prefix), axis=4)[::-1]
        fold_value = -pot_size[None, :, :, None] * opp_mass
        log_fold = jax.nn.log_sigmoid(-logits) + learning_rate * fold_value[..., None]
        acc_keep = jnp.zeros((2, LINES, BELIEFS, B), jnp.float32)
        acc_fold = jnp.full((2, LINES, BELIEFS, B), -jnp.inf, jnp.float32)
        updated = []
        for level in range(LEVELS - 1, -1, -1):
            next_value = jnp.logaddexp(acc_keep + learning_rate * target, acc_fold) / learning_rate
            updated.append(logits[:, level] + learning_rate * (next_value - fold_value[:, level][..., None]))
            acc_fold = jnp.logaddexp(keep[:, level] + acc_fold, log_fold[:, level])
            acc_keep = keep[:, level] + acc_keep
        logits = jnp.stack(updated[::-1], axis=1)
    return logits, utility
```

```python
import functools

import jax
import jax.numpy as jnp
from jax import lax
from jax.experimental import pallas as pl
from jax.experimental.pallas import tpu as pltpu
from jax.sharding import PartitionSpec as P

STEPS = 3
ROWS = 16
LANES = 128
MESH = pl.DeviceIdType.MESH


learning_rate = 1.0


def per_device(plan_logits, pot_size, payoff_tiles, parent_first, parent_second):
    logits = plan_logits
    line_count = logits.shape[2]
    level_index = lax.axis_index("narrow")
    line_ids = jnp.arange(line_count, dtype=jnp.int32)[None, :]
    pick_first = (parent_first[:, None] == line_ids).astype(jnp.bfloat16)
    pick_second = (parent_second[:, None] == line_ids).astype(jnp.bfloat16)
    sum_first = pick_first.astype(jnp.float32)
    sum_second = pick_second.astype(jnp.float32)
    previous = None
    utility = None
    for iteration in range(STEPS):
        keep = jax.nn.log_sigmoid(logits)
        local_keep = None
        local_fold = None
        every_logit, every_pot = (
            lax.all_gather(logits, "narrow", axis=1, tiled=True),
            lax.all_gather(pot_size, "narrow", axis=0, tiled=True),
        )
        every_keep = jax.nn.log_sigmoid(every_logit)
        every_prefix = jnp.cumsum(every_keep, axis=1) - every_keep
        reached = jnp.exp(jnp.sum(every_keep, axis=1)).astype(jnp.bfloat16)
        every_mass = jnp.mean(jnp.exp(every_prefix), axis=4)[::-1]
        every_fold = (-every_pot[None, :, :, None] * every_mass)[..., None]
        every_log_fold = jax.nn.log_sigmoid(-every_logit) + learning_rate * every_fold
        fold_value = lax.dynamic_slice_in_dim(every_fold, level_index, 1, 1)
        level_count = every_keep.shape[1]
        acc_keep = jnp.zeros_like(keep[:, 0])
        acc_fold = jnp.full_like(keep[:, 0], -jnp.inf)
        local_keep = jnp.zeros_like(keep[:, 0])
        local_fold = jnp.zeros_like(keep[:, 0])
        for level in range(level_count - 1, -1, -1):
            mine = level_index == level
            local_keep = jnp.where(mine, acc_keep, local_keep)
            local_fold = jnp.where(mine, acc_fold, local_fold)
            acc_fold = jnp.logaddexp(every_keep[:, level] + acc_fold, every_log_fold[:, level])
            acc_keep = every_keep[:, level] + acc_keep
        local_keep = local_keep[:, None]
        local_fold = local_fold[:, None]
        first_reach = jnp.einsum(
            "ls,sbj->lbj", pick_first, reached[0], preferred_element_type=jnp.float32
        ).astype(jnp.bfloat16)
        second_reach = jnp.einsum(
            "ls,sbj->lbj", pick_second, reached[1], preferred_element_type=jnp.float32
        ).astype(jnp.bfloat16)
        value_first = jnp.einsum(
            "lbj,lij->lbi", second_reach, payoff_tiles, preferred_element_type=jnp.float32
        )
        value_second = -jnp.einsum(
            "lbi,lij->lbj", first_reach, payoff_tiles, preferred_element_type=jnp.float32
        )
        local_sums = jnp.stack(
            [
                jnp.einsum("ls,lbi->sbi", sum_first, value_first, precision=lax.Precision.HIGHEST),
                jnp.einsum(
                    "ls,lbi->sbi", sum_second, value_second, precision=lax.Precision.HIGHEST
                ),
            ]
        )
        suffix_keep, suffix_fold = (local_keep, local_fold)
        utility = lax.psum(local_sums, ("wide", "narrow"))
        if previous is None:
            previous = utility
        target = 2.0 * utility - previous
        previous = utility
        next_value = (
            jnp.logaddexp(suffix_keep + learning_rate * target[:, None], suffix_fold)
            / learning_rate
        )
        logits = logits + learning_rate * (next_value - fold_value)
    return (logits, utility)


def softplus(x):
    return jnp.maximum(x, 0.0) + jnp.log(1.0 + jnp.exp(-jnp.abs(x)))


def wait_bytes(ref, sem):
    pltpu.make_async_copy(ref, ref, sem).wait()


def solve_kernel(
    wide,
    narrow,
    logits_ref,
    pot_ref,
    payoff_ref,
    first_ref,
    second_ref,
    logits_out,
    utility_out,
    state,
    soft,
    payoff,
    pots,
    parent,
    parents,
    reach,
    mass,
    fold,
    values,
    parts,
    sums,
    utility,
    level_sem,
    level_sent,
    pot_sem,
    pot_sent,
    parent_sem,
    parent_sent,
    payoff_sem,
    parts_sem,
    parts_sent,
    sums_sem,
    sums_sent,
    out_sem,
):
    devices = wide * narrow
    _, levels, lines, beliefs, buckets = state.shape
    own_levels = logits_ref.shape[1]
    halves = beliefs // ROWS
    tiles = devices // 2
    my_wide, my_narrow = lax.axis_index("wide"), lax.axis_index("narrow")
    me = my_wide * narrow + my_narrow
    my_levels = pl.ds(my_narrow * own_levels, own_levels)

    def at(device):
        return (lax.div(device, narrow), lax.rem(device, narrow))

    def remote(src, dst, sent, received, device):
        return pltpu.make_async_remote_copy(
            src_ref=src,
            dst_ref=dst,
            send_sem=sent,
            recv_sem=received,
            device_id=device,
            device_id_type=MESH,
        )

    pltpu.make_async_copy(logits_ref, state.at[:, my_levels], level_sem).start()
    pltpu.make_async_copy(payoff_ref.at[0], payoff, payoff_sem).start()

    barrier = pltpu.get_barrier_semaphore()

    @pl.loop(1, devices)
    def _(step):
        pl.semaphore_signal(
            barrier, inc=1, device_id=at(lax.rem(me + step, devices)), device_id_type=MESH
        )

    parent[0] = jnp.full((1, LANES), first_ref[0], jnp.int32)
    parent[1] = jnp.full((1, LANES), second_ref[0], jnp.int32)
    for level in range(own_levels):
        for line in range(lines):
            pots[my_narrow * own_levels + level, line] = jnp.broadcast_to(
                pot_ref[level : level + 1, line : line + 1], (8, LANES)
            )
    pl.semaphore_wait(barrier, devices - 1)

    for step in range(1, narrow):
        peer = (my_wide, lax.rem(my_narrow + step, narrow))
        remote(logits_ref, state.at[:, my_levels], level_sent, level_sem, peer).start()
        remote(pots.at[my_levels], pots.at[my_levels], pot_sent, pot_sem, peer).start()

    @pl.loop(1, devices)
    def _(step):
        other = lax.rem(me + step, devices)
        remote(
            parent.at[lax.rem(other, 2)], parents.at[me], parent_sent, parent_sem, at(other)
        ).start()

    pltpu.make_async_copy(parent.at[lax.rem(me, 2)], parents.at[me], parent_sem).start()

    def place(tile):
        half = lax.rem(tile, halves)
        chunk = lax.div(tile, halves)
        return (
            pl.ds(pl.multiple_of(half * ROWS, ROWS), ROWS),
            pl.ds(pl.multiple_of(chunk * LANES, LANES), LANES),
        )

    def finish_tile(player, rows, lanes, fresh):
        chosen = None
        for line in range(lines):
            total = None
            for level in range(levels):
                logit, plus = fresh[line][level]
                if level:
                    mass[player, level, line, rows] += jnp.exp(total)
                total = logit - plus if total is None else total + (logit - plus)
            if chosen is None:
                chosen = total
            else:
                picked = jnp.broadcast_to(parent[player], (ROWS, LANES)) == line
                chosen = jnp.where(picked, total, chosen)
        reach[player, rows, lanes] = jnp.exp(chosen).astype(jnp.bfloat16)

    def finish_fold():
        for player in range(2):
            for line in range(lines):
                for level in range(levels):
                    pot = pots[level, line, 0:1, :]
                    if level:
                        mean = jnp.sum(
                            mass[1 - player, level, line], axis=-1, keepdims=True
                        ) * (1.0 / buckets)
                        fold[player, level, line] = -(pot * mean)
                    else:
                        fold[player, level, line] = jnp.broadcast_to(-pot, (beliefs, LANES))

    def update(step, player, tile, last):
        rows, lanes = place(tile)
        unit = 2 * tile + player
        fresh = []
        for line in range(lines):
            now = utility[step, unit, line].astype(jnp.float32)
            value = now
            if step:
                value = 2.0 * now - utility[step - 1, unit, line].astype(jnp.float32)
            of_line = [None] * levels
            for level in range(levels - 1, -1, -1):
                here = (player, level, line, rows, lanes)
                lost = fold[player, level, line, rows]
                logit = state[here] + (value - lost)
                state[here] = logit
                if level or not last:
                    plus = softplus(logit)
                    value = lost + (plus - soft[here])
                    if not last:
                        soft[here] = plus
                        of_line[level] = (logit, plus)
            fresh.append(of_line)
            if last:
                sums_out[player, line, rows, lanes] = now
        if not last:
            finish_tile(player, rows, lanes, fresh)

    sums_out = utility_out

    wait_bytes(pots.at[pl.ds(0, levels - own_levels)], pot_sem)
    wait_bytes(state, level_sem)
    mass[...] = jnp.zeros_like(mass)
    for player in range(2):

        @pl.loop(0, tiles)
        def _(tile):
            rows, lanes = place(tile)
            fresh = []
            for line in range(lines):
                of_line = []
                for level in range(levels):
                    here = (player, level, line, rows, lanes)
                    logit = state[here]
                    plus = softplus(logit)
                    soft[here] = plus
                    of_line.append((logit, plus))
                fresh.append(of_line)
            finish_tile(player, rows, lanes, fresh)

    wait_bytes(payoff, payoff_sem)
    width = min(256, buckets)
    for step in range(STEPS):
        for player in range(2):
            for begin in range(0, buckets, width):
                if player == 0:
                    product = lax.dot_general(
                        reach[1],
                        payoff[begin : begin + width, :],
                        (((1,), (1,)), ((), ())),
                        preferred_element_type=jnp.float32,
                    )
                else:
                    product = -jnp.dot(
                        reach[0],
                        payoff[:, begin : begin + width],
                        preferred_element_type=jnp.float32,
                    )
                product = product.astype(jnp.bfloat16)
                for column in range(0, width, LANES):
                    for half in range(halves):
                        tile = (begin + column) // LANES * halves + half
                        values[step, 2 * tile + player] = product[
                            half * ROWS : (half + 1) * ROWS, column : column + LANES
                        ]

            @pl.loop(0, tiles)
            def _(index):
                unit = 2 * lax.rem(lax.div(me, 2) + index, tiles) + player

                @pl.when(unit != me)
                def _():
                    remote(
                        values.at[step, unit],
                        parts.at[step, me],
                        parts_sent.at[step],
                        parts_sem.at[step],
                        at(unit),
                    ).start()

                @pl.when(unit == me)
                def _():
                    pltpu.make_async_copy(
                        values.at[step, unit], parts.at[step, me], parts_sem.at[step]
                    ).start()

        finish_fold()
        mass[...] = jnp.zeros_like(mass)
        if step == 0:
            wait_bytes(parents, parent_sem)
        wait_bytes(parts.at[step], parts_sem.at[step])

        def add(device, totals):
            part = parts[step, device].astype(jnp.float32)
            owner = jnp.broadcast_to(parents[device], (ROWS, LANES))
            return tuple(
                total + jnp.where(owner == line, part, 0.0) for line, total in enumerate(totals)
            )

        zero = jnp.zeros((ROWS, LANES), jnp.float32)
        totals = lax.fori_loop(0, devices, add, (zero,) * lines, unroll=8)
        for line in range(lines):
            sums[step, line] = totals[line].astype(jnp.bfloat16)

        @pl.loop(1, devices)
        def _(index):
            other = lax.rem(me + index, devices)
            remote(
                sums.at[step],
                utility.at[step, me],
                sums_sent.at[step],
                sums_sem.at[step],
                at(other),
            ).start()

        pltpu.make_async_copy(sums.at[step], utility.at[step, me], sums_sem.at[step]).start()
        wait_bytes(utility.at[step], sums_sem.at[step])
        for player in range(2):

            @pl.loop(0, tiles)
            def _(tile):
                update(step, player, tile, step == STEPS - 1)

    out = pltpu.make_async_copy(state.at[:, my_levels], logits_out, out_sem)
    out.start()
    for _ in range(1, narrow):
        wait_bytes(state.at[:, my_levels], level_sent)
        wait_bytes(pots.at[my_levels], pot_sent)
    wait_bytes(parents.at[pl.ds(0, devices - 1)], parent_sent)
    for step in range(STEPS):
        wait_bytes(values.at[step, pl.ds(0, devices - 1)], parts_sent.at[step])
        wait_bytes(utility.at[step, pl.ds(0, devices - 1)], sums_sent.at[step])
    out.wait()


def solve(wide, narrow, plan_logits, pot_size, payoff_tiles, parent_first, parent_second):
    devices = wide * narrow
    players, own_levels, lines, beliefs, buckets = plan_logits.shape
    levels = own_levels * narrow
    whole = (players, levels, lines, beliefs, buckets)
    tile = (ROWS, LANES)
    dma = pltpu.SemaphoreType.DMA
    return pl.pallas_call(
        functools.partial(solve_kernel, wide, narrow),
        out_shape=(
            jax.ShapeDtypeStruct(plan_logits.shape, jnp.float32),
            jax.ShapeDtypeStruct((players, lines, beliefs, buckets), jnp.float32),
        ),
        in_specs=[
            pl.BlockSpec(memory_space=pl.ANY),
            pl.BlockSpec(memory_space=pltpu.VMEM),
            pl.BlockSpec(memory_space=pl.ANY),
            pl.BlockSpec(memory_space=pltpu.SMEM),
            pl.BlockSpec(memory_space=pltpu.SMEM),
        ],
        out_specs=(pl.BlockSpec(memory_space=pl.ANY), pl.BlockSpec(memory_space=pltpu.VMEM)),
        scratch_shapes=[
            pltpu.VMEM(whole, jnp.float32),
            pltpu.VMEM(whole, jnp.float32),
            pltpu.VMEM((buckets, buckets), jnp.bfloat16),
            pltpu.VMEM((levels, lines, 8, LANES), jnp.float32),
            pltpu.VMEM((players, 1, LANES), jnp.int32),
            pltpu.VMEM((devices, 1, LANES), jnp.int32),
            pltpu.VMEM((players, beliefs, buckets), jnp.bfloat16),
            pltpu.VMEM((players, levels, lines, beliefs, LANES), jnp.float32),
            pltpu.VMEM((players, levels, lines, beliefs, LANES), jnp.float32),
            pltpu.VMEM((STEPS, devices) + tile, jnp.bfloat16),
            pltpu.VMEM((STEPS, devices) + tile, jnp.bfloat16),
            pltpu.VMEM((STEPS, lines) + tile, jnp.bfloat16),
            pltpu.VMEM((STEPS, devices, lines) + tile, jnp.bfloat16),
            dma,
            dma,
            dma,
            dma,
            dma,
            dma,
            dma,
            dma((STEPS,)),
            dma((STEPS,)),
            dma((STEPS,)),
            dma((STEPS,)),
            dma,
        ],
        compiler_params=pltpu.CompilerParams(
            collective_id=0, has_side_effects=True, vmem_limit_bytes=32 * 1024 * 1024
        ),
    )(plan_logits, pot_size, payoff_tiles, parent_first, parent_second)


def choose(wide, narrow, *arrays):
    players, _, _, beliefs, buckets = arrays[0].shape
    units = players * (beliefs // ROWS) * (buckets // LANES)
    whole_tiles = beliefs % ROWS == 0 and buckets % LANES == 0
    if whole_tiles and units == wide * narrow and arrays[2].shape[0] == 1 and narrow > 1:
        return solve(wide, narrow, *arrays)
    return per_device(*arrays)


def solution(mesh):
    in_specs = (
        P(None, "narrow", None, None, None),
        P("narrow", None),
        P(("wide", "narrow"), None, None),
        P(("wide", "narrow")),
        P(("wide", "narrow")),
    )
    out_specs = (P(None, "narrow", None, None, None), P())
    return jax.shard_map(
        functools.partial(choose, mesh.shape["wide"], mesh.shape["narrow"]),
        mesh=mesh,
        in_specs=in_specs,
        out_specs=out_specs,
        check_vma=False,
    )
```

```python
import functools

import jax
import jax.numpy as jnp
from jax import lax
from jax.experimental import pallas as pl
from jax.experimental.pallas import tpu as pltpu
from jax.sharding import PartitionSpec as P

STEPS = 3
ROWS = 16
LANES = 128
SPAN = 256
WIRE = jnp.bfloat16
SCALE = 1.0
MESH = pl.DeviceIdType.MESH


learning_rate = 1.0


def per_device(plan_logits, pot_size, payoff_tiles, parent_first, parent_second):
    logits = plan_logits
    line_count = logits.shape[2]
    level_index = lax.axis_index("narrow")
    line_ids = jnp.arange(line_count, dtype=jnp.int32)[None, :]
    pick_first = (parent_first[:, None] == line_ids).astype(jnp.bfloat16)
    pick_second = (parent_second[:, None] == line_ids).astype(jnp.bfloat16)
    sum_first = pick_first.astype(jnp.float32)
    sum_second = pick_second.astype(jnp.float32)
    previous = None
    utility = None
    for iteration in range(STEPS):
        keep = jax.nn.log_sigmoid(logits)
        local_keep = None
        local_fold = None
        every_logit, every_pot = (
            lax.all_gather(logits, "narrow", axis=1, tiled=True),
            lax.all_gather(pot_size, "narrow", axis=0, tiled=True),
        )
        every_keep = jax.nn.log_sigmoid(every_logit)
        every_prefix = jnp.cumsum(every_keep, axis=1) - every_keep
        reached = jnp.exp(jnp.sum(every_keep, axis=1)).astype(jnp.bfloat16)
        every_mass = jnp.mean(jnp.exp(every_prefix), axis=4)[::-1]
        every_fold = (-every_pot[None, :, :, None] * every_mass)[..., None]
        every_log_fold = jax.nn.log_sigmoid(-every_logit) + learning_rate * every_fold
        fold_value = lax.dynamic_slice_in_dim(every_fold, level_index, 1, 1)
        level_count = every_keep.shape[1]
        acc_keep = jnp.zeros_like(keep[:, 0])
        acc_fold = jnp.full_like(keep[:, 0], -jnp.inf)
        local_keep = jnp.zeros_like(keep[:, 0])
        local_fold = jnp.zeros_like(keep[:, 0])
        for level in range(level_count - 1, -1, -1):
            mine = level_index == level
            local_keep = jnp.where(mine, acc_keep, local_keep)
            local_fold = jnp.where(mine, acc_fold, local_fold)
            acc_fold = jnp.logaddexp(every_keep[:, level] + acc_fold, every_log_fold[:, level])
            acc_keep = every_keep[:, level] + acc_keep
        local_keep = local_keep[:, None]
        local_fold = local_fold[:, None]
        first_reach = jnp.einsum(
            "ls,sbj->lbj", pick_first, reached[0], preferred_element_type=jnp.float32
        ).astype(jnp.bfloat16)
        second_reach = jnp.einsum(
            "ls,sbj->lbj", pick_second, reached[1], preferred_element_type=jnp.float32
        ).astype(jnp.bfloat16)
        value_first = jnp.einsum(
            "lbj,lij->lbi", second_reach, payoff_tiles, preferred_element_type=jnp.float32
        )
        value_second = -jnp.einsum(
            "lbi,lij->lbj", first_reach, payoff_tiles, preferred_element_type=jnp.float32
        )
        local_sums = jnp.stack(
            [
                jnp.einsum("ls,lbi->sbi", sum_first, value_first, precision=lax.Precision.HIGHEST),
                jnp.einsum(
                    "ls,lbi->sbi", sum_second, value_second, precision=lax.Precision.HIGHEST
                ),
            ]
        )
        suffix_keep, suffix_fold = (local_keep, local_fold)
        utility = lax.psum(local_sums, ("wide", "narrow"))
        if previous is None:
            previous = utility
        target = 2.0 * utility - previous
        previous = utility
        next_value = (
            jnp.logaddexp(suffix_keep + learning_rate * target[:, None], suffix_fold)
            / learning_rate
        )
        logits = logits + learning_rate * (next_value - fold_value)
    return (logits, utility)


def softplus(x):
    return jnp.maximum(x, 0.0) + jnp.log(1.0 + jnp.exp(-jnp.abs(x)))


def wait_bytes(ref, sem):
    pltpu.make_async_copy(ref, ref, sem).wait()


def solve_kernel(
    wide,
    logits_ref,
    pot_ref,
    payoff_ref,
    first_ref,
    second_ref,
    logits_out,
    utility_out,
    state,
    soft,
    payoff,
    pots,
    parent,
    parents,
    reach,
    mass,
    fold,
    values,
    parts,
    sums,
    utility,
    shown,
    level_sem,
    level_sent,
    pot_sem,
    pot_sent,
    parent_sem,
    parent_sent,
    payoff_sem,
    parts_sem,
    parts_sent,
    sums_sem,
    sums_sent,
    pass_sem,
    pass_sent,
    out_sem,
):
    narrow = 2
    devices = wide * narrow
    _, levels, lines, beliefs, buckets = state.shape
    own_levels = logits_ref.shape[1]
    halves = beliefs // ROWS
    my_wide, mine = lax.axis_index("wide"), lax.axis_index("narrow")
    other = 1 - mine
    me = my_wide * narrow + mine
    my_levels = pl.ds(mine * own_levels, own_levels)
    span = next(width for width in (SPAN, LANES) if buckets % width == 0)

    def remote(src, dst, sent, received, device):
        return pltpu.make_async_remote_copy(
            src_ref=src,
            dst_ref=dst,
            send_sem=sent,
            recv_sem=received,
            device_id=device,
            device_id_type=MESH,
        )

    def place(tile):
        half = lax.rem(tile, halves)
        chunk = lax.div(tile, halves)
        return (
            pl.ds(pl.multiple_of(half * ROWS, ROWS), ROWS),
            pl.ds(pl.multiple_of(chunk * LANES, LANES), LANES),
        )

    my_rows, my_lanes = place(my_wide)

    load = pltpu.make_async_copy(payoff_ref.at[0], payoff.at[0], payoff_sem)
    load.start()
    pltpu.make_async_copy(logits_ref, state.at[:, my_levels], level_sem).start()

    barrier = pltpu.get_barrier_semaphore()

    @pl.loop(1, devices)
    def _(step):
        device = lax.rem(me + step, devices)
        pl.semaphore_signal(
            barrier,
            inc=1,
            device_id=(lax.div(device, narrow), lax.rem(device, narrow)),
            device_id_type=MESH,
        )

    parent[0] = jnp.full((1, LANES), first_ref[0], jnp.int32)
    parent[1] = jnp.full((1, LANES), second_ref[0], jnp.int32)
    for level in range(own_levels):
        for line in range(lines):
            pots[mine * own_levels + level, line] = jnp.broadcast_to(
                pot_ref[level : level + 1, line : line + 1], (8, LANES)
            )
    mass[...] = jnp.zeros_like(mass)
    pl.semaphore_wait(barrier, devices - 1)

    sibling = (my_wide, other)
    level_copy = remote(logits_ref, state.at[:, my_levels], level_sent, level_sem, sibling)
    level_copy.start()
    pot_copy = remote(pots.at[my_levels], pots.at[my_levels], pot_sent, pot_sem, sibling)
    pot_copy.start()

    @pl.loop(0, wide)
    def _(step):
        w = lax.rem(my_wide + step, wide)
        remote(parent.at[other], parents.at[me], parent_sent, parent_sem, (w, other)).start()

    @pl.loop(1, wide)
    def _(step):
        w = lax.rem(my_wide + step, wide)
        remote(parent.at[mine], parents.at[me], parent_sent, parent_sem, (w, mine)).start()

    pltpu.make_async_copy(parent.at[mine], parents.at[me], parent_sem).start()

    load.wait()
    side = min(256, buckets)
    for row in range(0, buckets, side):
        for column in range(0, buckets, side):
            payoff[1, column : column + side, row : row + side] = payoff[
                0, row : row + side, column : column + side
            ].T
    wait_bytes(pots.at[pl.ds(0, levels - own_levels)], pot_sem)
    wait_bytes(state, level_sem)

    def finish_block(player, lanes, fresh):
        chosen = None
        for line in range(lines):
            total = None
            for level in range(levels):
                logit, plus = fresh[line][level]
                if level:
                    lost = jnp.exp(total)
                    part = lost[:, :LANES]
                    for column in range(LANES, span, LANES):
                        part = part + lost[:, column : column + LANES]
                    mass[player, level, line] += part
                total = logit - plus if total is None else total + (logit - plus)
            if chosen is None:
                chosen = total
            else:
                picked = jnp.broadcast_to(parent[player][:, :1], (beliefs, span)) == line
                chosen = jnp.where(picked, total, chosen)
        reach[player, :, lanes] = jnp.exp(chosen).astype(jnp.bfloat16)

    def finish_fold():
        for player in range(2):
            for line in range(lines):
                for level in range(levels):
                    pot = pots[level, line, 0:1, :]
                    if level:
                        mean = jnp.sum(
                            mass[1 - player, level, line], axis=-1, keepdims=True
                        ) * (1.0 / buckets)
                        fold[player, level, line] = -(pot * mean)
                    else:
                        fold[player, level, line] = jnp.broadcast_to(-pot, (beliefs, LANES))

    def begin(player):
        @pl.loop(0, buckets // span)
        def _(block):
            lanes = pl.ds(pl.multiple_of(block * span, span), span)
            fresh = []
            for line in range(lines):
                of_line = []
                for level in range(levels):
                    logit = state[player, level, line, :, lanes]
                    of_line.append((logit, softplus(logit)))
                fresh.append(of_line)
            for line in range(lines):
                for level in range(levels):
                    soft[player, level, line, :, lanes] = fresh[line][level][1]
            finish_block(player, lanes, fresh)

    def update(step, player):
        last = step == STEPS - 1

        @pl.loop(0, buckets // span)
        def _(block):
            lanes = pl.ds(pl.multiple_of(block * span, span), span)
            old, seen, lost = {}, {}, {}
            for line in range(lines):
                now = utility[step, player, line, :, lanes].astype(jnp.float32) * (1.0 / SCALE)
                seen[line] = now, now
                if step:
                    before = utility[step - 1, player, line, :, lanes].astype(jnp.float32)
                    seen[line] = now, 2.0 * now - before * (1.0 / SCALE)
                for level in range(levels):
                    here = (player, level, line, slice(None), lanes)
                    old[line, level] = state[here], soft[here]
                    lost[line, level] = jnp.concatenate(
                        [fold[player, level, line]] * (span // LANES), axis=1
                    )
            fresh = []
            for line in range(lines):
                value = seen[line][1]
                of_line = [None] * levels
                for level in range(levels - 1, -1, -1):
                    logit = old[line, level][0] + (value - lost[line, level])
                    plus = None
                    if level or not last:
                        plus = softplus(logit)
                        value = lost[line, level] + (plus - old[line, level][1])
                    of_line[level] = logit, plus
                fresh.append(of_line)
            for line in range(lines):
                for level in range(levels):
                    here = (player, level, line, slice(None), lanes)
                    state[here] = fresh[line][level][0]
                    if not last:
                        soft[here] = fresh[line][level][1]
                if last:
                    shown[player, line, :, lanes] = seen[line][0]
            if not last:
                finish_block(player, lanes, fresh)

    def respond(step, player):
        target = 1 - player
        factor = jnp.where(player == 0, -SCALE, SCALE).astype(jnp.float32)
        for start in range(0, buckets, side):
            product = jnp.dot(
                reach[player],
                payoff[player, :, start : start + side],
                preferred_element_type=jnp.float32,
            )
            values[step, target, :, start : start + side] = (product * factor).astype(WIRE)

    def send_part(step, target, w):
        rows, lanes = place(w)
        return (
            values.at[step, target, rows, lanes],
            parts.at[step, me],
            parts_sent.at[step],
            parts_sem.at[step],
            (w, target),
        )

    begin(mine)
    for step in range(STEPS):
        respond(step, mine)

        @pl.loop(0, wide)
        def _(index):
            w = lax.rem(my_wide + index, wide)
            remote(*send_part(step, other, w)).start()

        if step:
            wait_bytes(utility.at[step - 1, other], pass_sem.at[step - 1])
            update(step - 1, other)
        else:
            begin(other)
        respond(step, other)

        @pl.loop(1, wide)
        def _(index):
            w = lax.rem(my_wide + index, wide)
            remote(*send_part(step, mine, w)).start()

        own = values.at[step, mine, my_rows, my_lanes]
        pltpu.make_async_copy(own, parts.at[step, me], parts_sem.at[step]).start()
        finish_fold()
        mass[...] = jnp.zeros_like(mass)
        if step == 0:
            wait_bytes(parents, parent_sem)
        wait_bytes(parts.at[step], parts_sem.at[step])

        def add(device, totals):
            part = parts[step, device].astype(jnp.float32)
            owner = jnp.broadcast_to(parents[device], (ROWS, LANES))
            return tuple(
                total + jnp.where(owner == line, part, 0.0) for line, total in enumerate(totals)
            )

        zero = jnp.zeros((ROWS, LANES), jnp.float32)
        totals = lax.fori_loop(0, devices, add, (zero,) * lines, unroll=8)
        for line in range(lines):
            sums[step, line] = totals[line].astype(WIRE)

        here = utility.at[step, mine, :, my_rows, my_lanes]

        @pl.loop(1, wide)
        def _(index):
            w = lax.rem(my_wide + index, wide)
            remote(
                sums.at[step], here, sums_sent.at[step, index], sums_sem.at[step], (w, mine)
            ).start()

        pltpu.make_async_copy(sums.at[step], here, sums_sem.at[step]).start()
        half = utility.at[step, mine]
        wait_bytes(half, sums_sem.at[step])
        remote(half, half, pass_sent.at[step], pass_sem.at[step], sibling).start()
        update(step, mine)

    final = STEPS - 1
    outs = [
        pltpu.make_async_copy(
            state.at[player, my_levels], logits_out.at[player], out_sem.at[0, index]
        )
        for index, player in enumerate((mine, other))
    ] + [
        pltpu.make_async_copy(shown.at[player], utility_out.at[player], out_sem.at[1, index])
        for index, player in enumerate((mine, other))
    ]
    outs[0].start()
    outs[2].start()
    wait_bytes(utility.at[final, other], pass_sem.at[final])
    update(final, other)
    outs[1].start()
    outs[3].start()
    level_copy.wait_send()
    pot_copy.wait_send()
    wait_bytes(parents.at[pl.ds(0, devices - 1)], parent_sent)
    for step in range(STEPS):
        wait_bytes(parts.at[step, pl.ds(0, devices - 1)], parts_sent.at[step])
        wait_bytes(utility.at[step, mine], pass_sent.at[step])

        @pl.loop(1, wide)
        def _(index):
            wait_bytes(sums.at[step], sums_sent.at[step, index])

    for out in outs:
        out.wait()


def solve(wide, plan_logits, pot_size, payoff_tiles, parent_first, parent_second):
    devices = wide * 2
    players, own_levels, lines, beliefs, buckets = plan_logits.shape
    levels = own_levels * 2
    whole = (players, levels, lines, beliefs, buckets)
    tile = (ROWS, LANES)
    dma = pltpu.SemaphoreType.DMA
    return pl.pallas_call(
        functools.partial(solve_kernel, wide),
        out_shape=(
            jax.ShapeDtypeStruct(plan_logits.shape, jnp.float32),
            jax.ShapeDtypeStruct((players, lines, beliefs, buckets), jnp.float32),
        ),
        in_specs=[
            pl.BlockSpec(memory_space=pltpu.HBM),
            pl.BlockSpec(memory_space=pltpu.VMEM),
            pl.BlockSpec(memory_space=pltpu.HBM),
            pl.BlockSpec(memory_space=pltpu.SMEM),
            pl.BlockSpec(memory_space=pltpu.SMEM),
        ],
        out_specs=(
            pl.BlockSpec(memory_space=pl.ANY),
            pl.BlockSpec(memory_space=pl.ANY),
        ),
        scratch_shapes=[
            pltpu.VMEM(whole, jnp.float32),
            pltpu.VMEM(whole, jnp.float32),
            pltpu.VMEM((2, buckets, buckets), jnp.bfloat16),
            pltpu.VMEM((levels, lines, 8, LANES), jnp.float32),
            pltpu.VMEM((players, 1, LANES), jnp.int32),
            pltpu.VMEM((devices, 1, LANES), jnp.int32),
            pltpu.VMEM((players, beliefs, buckets), jnp.bfloat16),
            pltpu.VMEM((players, levels, lines, beliefs, LANES), jnp.float32),
            pltpu.VMEM((players, levels, lines, beliefs, LANES), jnp.float32),
            pltpu.VMEM((STEPS, players, beliefs, buckets), WIRE),
            pltpu.VMEM((STEPS, devices) + tile, WIRE),
            pltpu.VMEM((STEPS, lines) + tile, WIRE),
            pltpu.VMEM((STEPS, players, lines, beliefs, buckets), WIRE),
            pltpu.VMEM((players, lines, beliefs, buckets), jnp.float32),
            dma,
            dma,
            dma,
            dma,
            dma,
            dma,
            dma,
            dma((STEPS,)),
            dma((STEPS,)),
            dma((STEPS,)),
            dma((STEPS, wide)),
            dma((STEPS,)),
            dma((STEPS,)),
            dma((2, 2)),
        ],
        compiler_params=pltpu.CompilerParams(
            collective_id=0, has_side_effects=True, vmem_limit_bytes=32 * 1024 * 1024
        ),
    )(plan_logits, pot_size, payoff_tiles, parent_first, parent_second)


def choose(wide, narrow, *arrays):
    players, _, _, beliefs, buckets = arrays[0].shape
    units = players * (beliefs // ROWS) * (buckets // LANES)
    whole_tiles = beliefs % ROWS == 0 and buckets % LANES == 0
    if whole_tiles and units == wide * narrow and arrays[2].shape[0] == 1 and narrow == 2:
        return solve(wide, *arrays)
    return per_device(*arrays)


def solution(mesh):
    in_specs = (
        P(None, "narrow", None, None, None),
        P("narrow", None),
        P(("wide", "narrow"), None, None),
        P(("wide", "narrow")),
        P(("wide", "narrow")),
    )
    out_specs = (P(None, "narrow", None, None, None), P())
    return jax.shard_map(
        functools.partial(choose, mesh.shape["wide"], mesh.shape["narrow"]),
        mesh=mesh,
        in_specs=in_specs,
        out_specs=out_specs,
        check_vma=False,
    )
```

```python
import functools

import jax
import jax.numpy as jnp
from jax import lax
from jax.experimental import pallas as pl
from jax.experimental.pallas import tpu as pltpu
from jax.sharding import PartitionSpec as P

STEPS = 3
ROWS = 16
LANES = 128
SPAN = 256
WIRE = jnp.bfloat16
SCALE = 1.0
MESH = pl.DeviceIdType.MESH


learning_rate = 1.0


def per_device(plan_logits, pot_size, payoff_tiles, parent_first, parent_second):
    logits = plan_logits
    line_count = logits.shape[2]
    level_index = lax.axis_index("narrow")
    line_ids = jnp.arange(line_count, dtype=jnp.int32)[None, :]
    pick_first = (parent_first[:, None] == line_ids).astype(jnp.bfloat16)
    pick_second = (parent_second[:, None] == line_ids).astype(jnp.bfloat16)
    sum_first = pick_first.astype(jnp.float32)
    sum_second = pick_second.astype(jnp.float32)
    previous = None
    utility = None
    for iteration in range(STEPS):
        keep = jax.nn.log_sigmoid(logits)
        local_keep = None
        local_fold = None
        every_logit, every_pot = (
            lax.all_gather(logits, "narrow", axis=1, tiled=True),
            lax.all_gather(pot_size, "narrow", axis=0, tiled=True),
        )
        every_keep = jax.nn.log_sigmoid(every_logit)
        every_prefix = jnp.cumsum(every_keep, axis=1) - every_keep
        reached = jnp.exp(jnp.sum(every_keep, axis=1)).astype(jnp.bfloat16)
        every_mass = jnp.mean(jnp.exp(every_prefix), axis=4)[::-1]
        every_fold = (-every_pot[None, :, :, None] * every_mass)[..., None]
        every_log_fold = jax.nn.log_sigmoid(-every_logit) + learning_rate * every_fold
        fold_value = lax.dynamic_slice_in_dim(every_fold, level_index, 1, 1)
        level_count = every_keep.shape[1]
        acc_keep = jnp.zeros_like(keep[:, 0])
        acc_fold = jnp.full_like(keep[:, 0], -jnp.inf)
        local_keep = jnp.zeros_like(keep[:, 0])
        local_fold = jnp.zeros_like(keep[:, 0])
        for level in range(level_count - 1, -1, -1):
            mine = level_index == level
            local_keep = jnp.where(mine, acc_keep, local_keep)
            local_fold = jnp.where(mine, acc_fold, local_fold)
            acc_fold = jnp.logaddexp(every_keep[:, level] + acc_fold, every_log_fold[:, level])
            acc_keep = every_keep[:, level] + acc_keep
        local_keep = local_keep[:, None]
        local_fold = local_fold[:, None]
        first_reach = jnp.einsum(
            "ls,sbj->lbj", pick_first, reached[0], preferred_element_type=jnp.float32
        ).astype(jnp.bfloat16)
        second_reach = jnp.einsum(
            "ls,sbj->lbj", pick_second, reached[1], preferred_element_type=jnp.float32
        ).astype(jnp.bfloat16)
        value_first = jnp.einsum(
            "lbj,lij->lbi", second_reach, payoff_tiles, preferred_element_type=jnp.float32
        )
        value_second = -jnp.einsum(
            "lbi,lij->lbj", first_reach, payoff_tiles, preferred_element_type=jnp.float32
        )
        local_sums = jnp.stack(
            [
                jnp.einsum("ls,lbi->sbi", sum_first, value_first, precision=lax.Precision.HIGHEST),
                jnp.einsum(
                    "ls,lbi->sbi", sum_second, value_second, precision=lax.Precision.HIGHEST
                ),
            ]
        )
        suffix_keep, suffix_fold = (local_keep, local_fold)
        utility = lax.psum(local_sums, ("wide", "narrow"))
        if previous is None:
            previous = utility
        target = 2.0 * utility - previous
        previous = utility
        next_value = (
            jnp.logaddexp(suffix_keep + learning_rate * target[:, None], suffix_fold)
            / learning_rate
        )
        logits = logits + learning_rate * (next_value - fold_value)
    return (logits, utility)


def softplus(x):
    return jnp.maximum(x, 0.0) + jnp.log(1.0 + jnp.exp(-jnp.abs(x)))


def wait_bytes(ref, sem):
    pltpu.make_async_copy(ref, ref, sem).wait()


def solve_kernel(
    wide,
    logits_ref,
    pot_ref,
    payoff_ref,
    first_ref,
    second_ref,
    logits_out,
    utility_out,
    state,
    soft,
    payoff,
    pots,
    parent,
    parents,
    reach,
    mass,
    fold,
    values,
    parts,
    sums,
    utility,
    shown,
    running,
    level_sem,
    level_sent,
    pot_sem,
    pot_sent,
    parent_sem,
    parent_sent,
    payoff_sem,
    parts_sem,
    parts_sent,
    sums_sem,
    sums_sent,
    pass_sem,
    pass_sent,
    out_sem,
):
    narrow = 2
    devices = wide * narrow
    _, levels, lines, beliefs, buckets = state.shape
    own_levels = logits_ref.shape[1]
    halves = beliefs // ROWS
    my_wide, mine = lax.axis_index("wide"), lax.axis_index("narrow")
    other = 1 - mine
    me = my_wide * narrow + mine
    my_levels = pl.ds(mine * own_levels, own_levels)
    span = next(width for width in (SPAN, LANES) if buckets % width == 0)

    def remote(src, dst, sent, received, device):
        return pltpu.make_async_remote_copy(
            src_ref=src,
            dst_ref=dst,
            send_sem=sent,
            recv_sem=received,
            device_id=device,
            device_id_type=MESH,
        )

    def place(tile):
        half = lax.rem(tile, halves)
        chunk = lax.div(tile, halves)
        return (
            pl.ds(pl.multiple_of(half * ROWS, ROWS), ROWS),
            pl.ds(pl.multiple_of(chunk * LANES, LANES), LANES),
        )

    my_rows, my_lanes = place(my_wide)
    blocks = buckets // span
    owners = wide // blocks
    my_block = lax.div(my_wide, owners)
    toward = 1 - 2 * lax.rem(my_block, 2)

    def lanes_of(block):
        return pl.ds(pl.multiple_of(block * span, span), span)

    def nearest(index):
        return lax.rem(my_block + index * toward + blocks, blocks)

    load = pltpu.make_async_copy(payoff_ref.at[0], payoff.at[0], payoff_sem)
    load.start()
    for player in (mine, other):
        pltpu.make_async_copy(
            logits_ref.at[player], state.at[player, my_levels], level_sem.at[player]
        ).start()

    barrier = pltpu.get_barrier_semaphore()

    @pl.loop(1, devices)
    def _(step):
        device = lax.rem(me + step, devices)
        pl.semaphore_signal(
            barrier,
            inc=1,
            device_id=(lax.div(device, narrow), lax.rem(device, narrow)),
            device_id_type=MESH,
        )

    parent[0] = jnp.full((1, LANES), first_ref[0], jnp.int32)
    parent[1] = jnp.full((1, LANES), second_ref[0], jnp.int32)
    for level in range(own_levels):
        for line in range(lines):
            pots[mine * own_levels + level, line] = jnp.full(
                (8, LANES), pot_ref[level, line], jnp.float32
            )
    mass[...] = jnp.zeros_like(mass)
    pl.semaphore_wait(barrier, devices - 1)

    sibling = (my_wide, other)
    level_copies = [
        remote(
            logits_ref.at[player],
            state.at[player, my_levels],
            level_sent.at[player],
            level_sem.at[player],
            sibling,
        )
        for player in (other, mine)
    ]
    for copy in level_copies:
        copy.start()
    pot_copy = remote(pots.at[my_levels], pots.at[my_levels], pot_sent, pot_sem, sibling)
    pot_copy.start()

    @pl.loop(0, wide)
    def _(step):
        w = lax.rem(my_wide + step, wide)
        remote(parent.at[other], parents.at[mine, my_wide], parent_sent, parent_sem, (w, other)).start()

    @pl.loop(1, wide)
    def _(step):
        w = lax.rem(my_wide + step, wide)
        remote(parent.at[mine], parents.at[mine, my_wide], parent_sent, parent_sem, (w, mine)).start()

    pltpu.make_async_copy(parent.at[mine], parents.at[mine, my_wide], parent_sem).start()

    load.wait()
    side = min(256, buckets)
    for row in range(0, buckets, side):
        for column in range(0, buckets, side):
            payoff[1, column : column + side, row : row + side] = payoff[
                0, row : row + side, column : column + side
            ].T
    wait_bytes(pots.at[pl.ds(0, levels - own_levels)], pot_sem)

    def finish_block(player, lanes, fresh):
        chosen = None
        for line in range(lines):
            total = None
            for level in range(levels):
                logit, plus = fresh[line][level]
                if level:
                    lost = jnp.exp(total)
                    part = lost[:, :LANES]
                    for column in range(LANES, span, LANES):
                        part = part + lost[:, column : column + LANES]
                    mass[player, level, line] += part
                total = logit - plus if total is None else total + (logit - plus)
            if chosen is None:
                chosen = total
            else:
                picked = jnp.broadcast_to(parent[player][:, :1], (beliefs, span)) == line
                chosen = jnp.where(picked, total, chosen)
        reach[player, :, lanes] = jnp.exp(chosen).astype(jnp.bfloat16)

    def finish_fold():
        for player in range(2):
            for line in range(lines):
                for level in range(levels):
                    pot = pots[level, line, 0:1, :]
                    if level:
                        mean = jnp.sum(
                            mass[1 - player, level, line], axis=-1, keepdims=True
                        ) * (1.0 / buckets)
                        fold[player, level, line] = -(pot * mean)
                    else:
                        fold[player, level, line] = jnp.broadcast_to(-pot, (beliefs, LANES))

    def respond(player, lanes):
        width = min(512, buckets)
        for start in range(0, buckets, width):
            running[:, start : start + width] += jnp.dot(
                reach[player, :, lanes],
                payoff[player, lanes, start : start + width],
                preferred_element_type=jnp.float32,
            )

    def begin(player):
        wait_bytes(state.at[player], level_sem.at[player])
        running[...] = jnp.zeros_like(running)

        @pl.loop(0, blocks)
        def _(block):
            lanes = lanes_of(block)
            fresh = []
            for line in range(lines):
                of_line = []
                for level in range(levels):
                    logit = state[player, level, line, :, lanes]
                    of_line.append((logit, softplus(logit)))
                fresh.append(of_line)
            for line in range(lines):
                for level in range(levels):
                    soft[player, level, line, :, lanes] = fresh[line][level][1]
            finish_block(player, lanes, fresh)
            respond(player, lanes)

    def update(step, player, forward):
        last = step == STEPS - 1
        running[...] = jnp.zeros_like(running)

        @pl.loop(0, blocks)
        def _(index):
            block = nearest(index)
            lanes = lanes_of(block)
            arrived = utility.at[step, player, :, :, lanes]
            if forward:
                wait_bytes(arrived, sums_sem.at[step, block])
                remote(
                    arrived, arrived, pass_sent.at[step, block], pass_sem.at[step, block], sibling
                ).start()
            else:
                wait_bytes(arrived, pass_sem.at[step, block])
            old, seen, lost = {}, {}, {}
            for line in range(lines):
                now = utility[step, player, line, :, lanes].astype(jnp.float32) * (1.0 / SCALE)
                seen[line] = now, now
                if step:
                    before = utility[step - 1, player, line, :, lanes].astype(jnp.float32)
                    seen[line] = now, 2.0 * now - before * (1.0 / SCALE)
                for level in range(levels):
                    here = (player, level, line, slice(None), lanes)
                    old[line, level] = state[here], soft[here]
                    lost[line, level] = jnp.concatenate(
                        [fold[player, level, line]] * (span // LANES), axis=1
                    )
            fresh = []
            for line in range(lines):
                value = seen[line][1]
                of_line = [None] * levels
                for level in range(levels - 1, -1, -1):
                    logit = old[line, level][0] + (value - lost[line, level])
                    plus = None
                    if level or not last:
                        plus = softplus(logit)
                        value = lost[line, level] + (plus - old[line, level][1])
                    of_line[level] = logit, plus
                fresh.append(of_line)
            for line in range(lines):
                for level in range(levels):
                    here = (player, level, line, slice(None), lanes)
                    state[here] = fresh[line][level][0]
                    if not last:
                        soft[here] = fresh[line][level][1]
                if last:
                    shown[player, line, :, lanes] = seen[line][0]
            if not last:
                finish_block(player, lanes, fresh)
                respond(player, lanes)

    def answer(step, player):
        target = 1 - player
        factor = jnp.where(player == 0, -SCALE, SCALE).astype(jnp.float32)
        values[step, target] = (running[...] * factor).astype(WIRE)

    def send_part(step, target, w):
        rows, lanes = place(w)
        return (
            values.at[step, target, rows, lanes],
            parts.at[step, mine, my_wide],
            parts_sent.at[step],
            parts_sem.at[step, mine],
            (w, target),
        )

    begin(mine)
    for step in range(STEPS):
        answer(step, mine)

        @pl.loop(0, wide)
        def _(index):
            w = lax.rem(my_wide + index, wide)
            remote(*send_part(step, other, w)).start()

        if step:
            update(step - 1, other, False)
        else:
            begin(other)
        answer(step, other)

        @pl.loop(1, wide)
        def _(index):
            w = lax.rem(my_wide + index, wide)
            remote(*send_part(step, mine, w)).start()

        own = values.at[step, mine, my_rows, my_lanes]
        pltpu.make_async_copy(
            own, parts.at[step, mine, my_wide], parts_sem.at[step, mine]
        ).start()
        finish_fold()
        mass[...] = jnp.zeros_like(mass)
        if step == 0:
            wait_bytes(parents, parent_sem)
        totals = (jnp.zeros((ROWS, LANES), jnp.float32),) * lines
        for core in (other, mine):
            wait_bytes(parts.at[step, core], parts_sem.at[step, core])

            def add(w, totals):
                part = parts[step, core, w].astype(jnp.float32)
                owner = jnp.broadcast_to(parents[core, w], (ROWS, LANES))
                return tuple(
                    total + jnp.where(owner == line, part, 0.0)
                    for line, total in enumerate(totals)
                )

            totals = lax.fori_loop(0, wide, add, totals, unroll=8)
        for line in range(lines):
            sums[step, line] = totals[line].astype(WIRE)

        here = utility.at[step, mine, :, my_rows, my_lanes]

        @pl.loop(1, wide)
        def _(index):
            w = lax.rem(my_wide + index * toward + wide, wide)
            remote(
                sums.at[step], here, sums_sent.at[step, index], sums_sem.at[step, my_block], (w, mine)
            ).start()

        pltpu.make_async_copy(sums.at[step], here, sums_sem.at[step, my_block]).start()
        update(step, mine, True)

    final = STEPS - 1
    outs = [
        pltpu.make_async_copy(
            state.at[player, my_levels], logits_out.at[player], out_sem.at[0, index]
        )
        for index, player in enumerate((mine, other))
    ] + [
        pltpu.make_async_copy(shown.at[player], utility_out.at[player], out_sem.at[1, index])
        for index, player in enumerate((mine, other))
    ]
    outs[0].start()
    outs[2].start()
    update(final, other, False)
    outs[1].start()
    outs[3].start()
    for copy in level_copies:
        copy.wait_send()
    pot_copy.wait_send()
    for core, count in enumerate((wide, wide - 1)):
        wait_bytes(parents.at[core, pl.ds(0, count)], parent_sent)
    for step in range(STEPS):
        for core, count in enumerate((wide, wide - 1)):
            wait_bytes(parts.at[step, core, pl.ds(0, count)], parts_sent.at[step])

        @pl.loop(0, blocks)
        def _(block):
            wait_bytes(utility.at[step, mine, :, :, lanes_of(block)], pass_sent.at[step, block])

        @pl.loop(1, wide)
        def _(index):
            wait_bytes(sums.at[step], sums_sent.at[step, index])

    for out in outs:
        out.wait()


def solve(wide, plan_logits, pot_size, payoff_tiles, parent_first, parent_second):
    devices = wide * 2
    players, own_levels, lines, beliefs, buckets = plan_logits.shape
    levels = own_levels * 2
    whole = (players, levels, lines, beliefs, buckets)
    tile = (ROWS, LANES)
    blocks = buckets // next(width for width in (SPAN, LANES) if buckets % width == 0)
    dma = pltpu.SemaphoreType.DMA
    return pl.pallas_call(
        functools.partial(solve_kernel, wide),
        out_shape=(
            jax.ShapeDtypeStruct(plan_logits.shape, jnp.float32),
            jax.ShapeDtypeStruct((players, lines, beliefs, buckets), jnp.float32),
        ),
        in_specs=[
            pl.BlockSpec(memory_space=pltpu.HBM),
            pl.BlockSpec(memory_space=pltpu.SMEM),
            pl.BlockSpec(memory_space=pltpu.HBM),
            pl.BlockSpec(memory_space=pltpu.SMEM),
            pl.BlockSpec(memory_space=pltpu.SMEM),
        ],
        out_specs=(
            pl.BlockSpec(memory_space=pl.ANY),
            pl.BlockSpec(memory_space=pl.ANY),
        ),
        scratch_shapes=[
            pltpu.VMEM(whole, jnp.float32),
            pltpu.VMEM(whole, jnp.float32),
            pltpu.VMEM((2, buckets, buckets), jnp.bfloat16),
            pltpu.VMEM((levels, lines, 8, LANES), jnp.float32),
            pltpu.VMEM((players, 1, LANES), jnp.int32),
            pltpu.VMEM((2, wide, 1, LANES), jnp.int32),
            pltpu.VMEM((players, beliefs, buckets), jnp.bfloat16),
            pltpu.VMEM((players, levels, lines, beliefs, LANES), jnp.float32),
            pltpu.VMEM((players, levels, lines, beliefs, LANES), jnp.float32),
            pltpu.VMEM((STEPS, players, beliefs, buckets), WIRE),
            pltpu.VMEM((STEPS, 2, wide) + tile, WIRE),
            pltpu.VMEM((STEPS, lines) + tile, WIRE),
            pltpu.VMEM((STEPS, players, lines, beliefs, buckets), WIRE),
            pltpu.VMEM((players, lines, beliefs, buckets), jnp.float32),
            pltpu.VMEM((beliefs, buckets), jnp.float32),
            dma((2,)),
            dma((2,)),
            dma,
            dma,
            dma,
            dma,
            dma,
            dma((STEPS, 2)),
            dma((STEPS,)),
            dma((STEPS, blocks)),
            dma((STEPS, wide)),
            dma((STEPS, blocks)),
            dma((STEPS, blocks)),
            dma((2, 2)),
        ],
        compiler_params=pltpu.CompilerParams(
            collective_id=0, has_side_effects=True, vmem_limit_bytes=60 * 1024 * 1024
        ),
    )(plan_logits, pot_size, payoff_tiles, parent_first, parent_second)


def choose(wide, narrow, *arrays):
    players, _, _, beliefs, buckets = arrays[0].shape
    units = players * (beliefs // ROWS) * (buckets // LANES)
    whole_tiles = beliefs % ROWS == 0 and buckets % LANES == 0
    if whole_tiles and units == wide * narrow and arrays[2].shape[0] == 1 and narrow == 2:
        return solve(wide, *arrays)
    return per_device(*arrays)


def solution(mesh):
    in_specs = (
        P(None, "narrow", None, None, None),
        P("narrow", None),
        P(("wide", "narrow"), None, None),
        P(("wide", "narrow")),
        P(("wide", "narrow")),
    )
    out_specs = (P(None, "narrow", None, None, None), P())
    return jax.shard_map(
        functools.partial(choose, mesh.shape["wide"], mesh.shape["narrow"]),
        mesh=mesh,
        in_specs=in_specs,
        out_specs=out_specs,
        check_vma=False,
    )
```

```python
import functools

import jax
import jax.numpy as jnp
from jax import lax
from jax.experimental import pallas as pl
from jax.experimental.pallas import tpu as pltpu
from jax.sharding import PartitionSpec as P

STEPS = 3
ROWS = 16
LANES = 128
SPAN = 256
WIRE = jnp.bfloat16
SCALE = 1.0
MESH = pl.DeviceIdType.MESH


learning_rate = 1.0


def per_device(plan_logits, pot_size, payoff_tiles, parent_first, parent_second):
    logits = plan_logits
    line_count = logits.shape[2]
    level_index = lax.axis_index("narrow")
    line_ids = jnp.arange(line_count, dtype=jnp.int32)[None, :]
    pick_first = (parent_first[:, None] == line_ids).astype(jnp.bfloat16)
    pick_second = (parent_second[:, None] == line_ids).astype(jnp.bfloat16)
    sum_first = pick_first.astype(jnp.float32)
    sum_second = pick_second.astype(jnp.float32)
    previous = None
    utility = None
    for iteration in range(STEPS):
        keep = jax.nn.log_sigmoid(logits)
        local_keep = None
        local_fold = None
        every_logit, every_pot = (
            lax.all_gather(logits, "narrow", axis=1, tiled=True),
            lax.all_gather(pot_size, "narrow", axis=0, tiled=True),
        )
        every_keep = jax.nn.log_sigmoid(every_logit)
        every_prefix = jnp.cumsum(every_keep, axis=1) - every_keep
        reached = jnp.exp(jnp.sum(every_keep, axis=1)).astype(jnp.bfloat16)
        every_mass = jnp.mean(jnp.exp(every_prefix), axis=4)[::-1]
        every_fold = (-every_pot[None, :, :, None] * every_mass)[..., None]
        every_log_fold = jax.nn.log_sigmoid(-every_logit) + learning_rate * every_fold
        fold_value = lax.dynamic_slice_in_dim(every_fold, level_index, 1, 1)
        level_count = every_keep.shape[1]
        acc_keep = jnp.zeros_like(keep[:, 0])
        acc_fold = jnp.full_like(keep[:, 0], -jnp.inf)
        local_keep = jnp.zeros_like(keep[:, 0])
        local_fold = jnp.zeros_like(keep[:, 0])
        for level in range(level_count - 1, -1, -1):
            mine = level_index == level
            local_keep = jnp.where(mine, acc_keep, local_keep)
            local_fold = jnp.where(mine, acc_fold, local_fold)
            acc_fold = jnp.logaddexp(every_keep[:, level] + acc_fold, every_log_fold[:, level])
            acc_keep = every_keep[:, level] + acc_keep
        local_keep = local_keep[:, None]
        local_fold = local_fold[:, None]
        first_reach = jnp.einsum(
            "ls,sbj->lbj", pick_first, reached[0], preferred_element_type=jnp.float32
        ).astype(jnp.bfloat16)
        second_reach = jnp.einsum(
            "ls,sbj->lbj", pick_second, reached[1], preferred_element_type=jnp.float32
        ).astype(jnp.bfloat16)
        value_first = jnp.einsum(
            "lbj,lij->lbi", second_reach, payoff_tiles, preferred_element_type=jnp.float32
        )
        value_second = -jnp.einsum(
            "lbi,lij->lbj", first_reach, payoff_tiles, preferred_element_type=jnp.float32
        )
        local_sums = jnp.stack(
            [
                jnp.einsum("ls,lbi->sbi", sum_first, value_first, precision=lax.Precision.HIGHEST),
                jnp.einsum(
                    "ls,lbi->sbi", sum_second, value_second, precision=lax.Precision.HIGHEST
                ),
            ]
        )
        suffix_keep, suffix_fold = (local_keep, local_fold)
        utility = lax.psum(local_sums, ("wide", "narrow"))
        if previous is None:
            previous = utility
        target = 2.0 * utility - previous
        previous = utility
        next_value = (
            jnp.logaddexp(suffix_keep + learning_rate * target[:, None], suffix_fold)
            / learning_rate
        )
        logits = logits + learning_rate * (next_value - fold_value)
    return (logits, utility)


def softplus(x):
    return jnp.maximum(x, 0.0) + jnp.log(1.0 + jnp.exp(-jnp.abs(x)))


def wait_bytes(ref, sem):
    pltpu.make_async_copy(ref, ref, sem).wait()


def solve_kernel(
    wide,
    logits_ref,
    pot_ref,
    payoff_ref,
    first_ref,
    second_ref,
    logits_out,
    utility_out,
    state,
    soft,
    payoff,
    pots,
    parent,
    parents,
    reach,
    mass,
    fold,
    values,
    parts,
    partial,
    gathered,
    sums,
    utility,
    shown,
    running,
    level_sem,
    level_sent,
    pot_sem,
    pot_sent,
    parent_sem,
    parent_sent,
    payoff_sem,
    parts_sem,
    parts_sent,
    partial_sem,
    partial_sent,
    sums_sem,
    sums_sent,
    pass_sem,
    pass_sent,
    out_sem,
):
    narrow = 2
    devices = wide * narrow
    _, levels, lines, beliefs, buckets = state.shape
    own_levels = logits_ref.shape[1]
    halves = beliefs // ROWS
    my_wide, mine = lax.axis_index("wide"), lax.axis_index("narrow")
    other = 1 - mine
    me = my_wide * narrow + mine
    my_levels = pl.ds(mine * own_levels, own_levels)
    span = next(width for width in (SPAN, LANES) if buckets % width == 0)

    def remote(src, dst, sent, received, device):
        return pltpu.make_async_remote_copy(
            src_ref=src,
            dst_ref=dst,
            send_sem=sent,
            recv_sem=received,
            device_id=device,
            device_id_type=MESH,
        )

    blocks = buckets // span
    owners = wide // blocks
    my_block, my_row = lax.rem(my_wide, blocks), lax.div(my_wide, blocks)

    def across(step):
        return my_row * blocks + lax.rem(my_block + step, blocks)

    def along(step):
        return lax.rem(my_wide + step * blocks, wide)

    my_rows = pl.ds(pl.multiple_of(lax.rem(my_row, halves) * ROWS, ROWS), ROWS)
    my_lanes = pl.ds(
        pl.multiple_of(my_block * span + lax.div(my_row, halves) * LANES, LANES), LANES
    )

    def lanes_of(block):
        return pl.ds(pl.multiple_of(block * span, span), span)

    def nearest(index):
        return lax.rem(my_block + index, blocks)

    load = pltpu.make_async_copy(payoff_ref.at[0], payoff.at[0], payoff_sem)
    load.start()
    for player in (mine, other):
        pltpu.make_async_copy(
            logits_ref.at[player], state.at[player, my_levels], level_sem.at[player]
        ).start()

    barrier = pltpu.get_barrier_semaphore()

    def greet(device):
        pl.semaphore_signal(barrier, inc=1, device_id=device, device_id_type=MESH)

    for step in range(blocks):
        greet((across(step), other))
        if step:
            greet((across(step), mine))
    for step in range(1, owners):
        greet((along(step), mine))

    parent[0] = jnp.full((1, LANES), first_ref[0], jnp.int32)
    parent[1] = jnp.full((1, LANES), second_ref[0], jnp.int32)
    for level in range(own_levels):
        for line in range(lines):
            pots[mine * own_levels + level, line] = jnp.full(
                (8, LANES), pot_ref[level, line], jnp.float32
            )
    mass[...] = jnp.zeros_like(mass)
    pl.semaphore_wait(barrier, 2 * blocks - 1 + owners - 1)

    sibling = (my_wide, other)
    level_copies = [
        remote(
            logits_ref.at[player],
            state.at[player, my_levels],
            level_sent.at[player],
            level_sem.at[player],
            sibling,
        )
        for player in (other, mine)
    ]
    for copy in level_copies:
        copy.start()
    pot_copy = remote(pots.at[my_levels], pots.at[my_levels], pot_sent, pot_sem, sibling)
    pot_copy.start()

    for step in range(blocks):
        for core in (other, mine) if step else (other,):
            remote(
                parent.at[core],
                parents.at[mine, my_block],
                parent_sent,
                parent_sem,
                (across(step), core),
            ).start()
    pltpu.make_async_copy(parent.at[mine], parents.at[mine, my_block], parent_sem).start()

    load.wait()
    side = min(256, buckets)
    for row in range(0, buckets, side):
        for column in range(0, buckets, side):
            payoff[1, column : column + side, row : row + side] = payoff[
                0, row : row + side, column : column + side
            ].T
    wait_bytes(pots.at[pl.ds(0, levels - own_levels)], pot_sem)

    def finish_block(player, lanes, fresh):
        chosen = None
        for line in range(lines):
            total = None
            for level in range(levels):
                logit, plus = fresh[line][level]
                if level:
                    lost = jnp.exp(total)
                    part = lost[:, :LANES]
                    for column in range(LANES, span, LANES):
                        part = part + lost[:, column : column + LANES]
                    mass[player, level, line] += part
                total = logit - plus if total is None else total + (logit - plus)
            if chosen is None:
                chosen = total
            else:
                picked = jnp.broadcast_to(parent[player][:, :1], (beliefs, span)) == line
                chosen = jnp.where(picked, total, chosen)
        reach[player, :, lanes] = jnp.exp(chosen).astype(jnp.bfloat16)

    def finish_fold():
        for player in range(2):
            for line in range(lines):
                for level in range(levels):
                    pot = pots[level, line, 0:1, :]
                    if level:
                        mean = jnp.sum(
                            mass[1 - player, level, line], axis=-1, keepdims=True
                        ) * (1.0 / buckets)
                        fold[player, level, line] = -(pot * mean)
                    else:
                        fold[player, level, line] = jnp.broadcast_to(-pot, (beliefs, LANES))

    def respond(player, lanes):
        width = min(512, buckets)
        for start in range(0, buckets, width):
            running[:, start : start + width] += jnp.dot(
                reach[player, :, lanes],
                payoff[player, lanes, start : start + width],
                preferred_element_type=jnp.float32,
            )

    def begin(player):
        wait_bytes(state.at[player], level_sem.at[player])
        running[...] = jnp.zeros_like(running)

        @pl.loop(0, blocks)
        def _(block):
            lanes = lanes_of(block)
            fresh = []
            for line in range(lines):
                of_line = []
                for level in range(levels):
                    logit = state[player, level, line, :, lanes]
                    of_line.append((logit, softplus(logit)))
                fresh.append(of_line)
            for line in range(lines):
                for level in range(levels):
                    soft[player, level, line, :, lanes] = fresh[line][level][1]
            finish_block(player, lanes, fresh)
            respond(player, lanes)

    def update(step, player, forward):
        last = step == STEPS - 1
        running[...] = jnp.zeros_like(running)

        @pl.loop(0, blocks)
        def _(index):
            block = nearest(index)
            lanes = lanes_of(block)
            arrived = utility.at[step, player, :, :, lanes]
            if forward:
                wait_bytes(arrived, sums_sem.at[step, block])

                @pl.when(index == 0)
                def _():
                    for hop in range(1, blocks):
                        mine_now = utility.at[step, mine, :, :, lanes_of(my_block)]
                        remote(
                            mine_now,
                            mine_now,
                            sums_sent.at[step, owners + hop],
                            sums_sem.at[step, my_block],
                            (across(hop), mine),
                        ).start()

                remote(
                    arrived, arrived, pass_sent.at[step, block], pass_sem.at[step, block], sibling
                ).start()
            else:
                wait_bytes(arrived, pass_sem.at[step, block])
            old, seen, lost = {}, {}, {}
            for line in range(lines):
                now = utility[step, player, line, :, lanes].astype(jnp.float32) * (1.0 / SCALE)
                seen[line] = now, now
                if step:
                    before = utility[step - 1, player, line, :, lanes].astype(jnp.float32)
                    seen[line] = now, 2.0 * now - before * (1.0 / SCALE)
                for level in range(levels):
                    here = (player, level, line, slice(None), lanes)
                    old[line, level] = state[here], soft[here]
                    lost[line, level] = jnp.concatenate(
                        [fold[player, level, line]] * (span // LANES), axis=1
                    )
            fresh = []
            for line in range(lines):
                value = seen[line][1]
                of_line = [None] * levels
                for level in range(levels - 1, -1, -1):
                    logit = old[line, level][0] + (value - lost[line, level])
                    plus = None
                    if level or not last:
                        plus = softplus(logit)
                        value = lost[line, level] + (plus - old[line, level][1])
                    of_line[level] = logit, plus
                fresh.append(of_line)
            for line in range(lines):
                for level in range(levels):
                    here = (player, level, line, slice(None), lanes)
                    state[here] = fresh[line][level][0]
                    if not last:
                        soft[here] = fresh[line][level][1]
                if last:
                    shown[player, line, :, lanes] = seen[line][0]
            if not last:
                finish_block(player, lanes, fresh)
                respond(player, lanes)

    def answer(step, player):
        target = 1 - player
        factor = jnp.where(player == 0, -SCALE, SCALE).astype(jnp.float32)
        values[step, target] = (running[...] * factor).astype(WIRE)

    def send_part(step, target, index):
        w = across(index)
        return remote(
            values.at[step, target, :, lanes_of(lax.rem(w, blocks))],
            parts.at[step, mine, my_block],
            parts_sent.at[step],
            parts_sem.at[step, mine],
            (w, target),
        )

    begin(mine)
    for step in range(STEPS):
        answer(step, mine)

        for index in range(blocks):
            send_part(step, other, index).start()

        if step:
            update(step - 1, other, False)
        else:
            begin(other)
        answer(step, other)

        for index in range(1, blocks):
            send_part(step, mine, index).start()
        own = values.at[step, mine, :, lanes_of(my_block)]
        pltpu.make_async_copy(
            own, parts.at[step, mine, my_block], parts_sem.at[step, mine]
        ).start()
        finish_fold()
        mass[...] = jnp.zeros_like(mass)
        if step == 0:
            wait_bytes(parents, parent_sem)
        totals = [None] * lines
        for core in (other, mine):
            wait_bytes(parts.at[step, core], parts_sem.at[step, core])
            for column in range(blocks):
                part = parts[step, core, column].astype(jnp.float32)
                owner = jnp.broadcast_to(parents[core, column][:, :1], (beliefs, span))
                for line in range(lines):
                    term = jnp.where(owner == line, part, 0.0)
                    totals[line] = term if totals[line] is None else totals[line] + term
        for row in range(owners):
            top, left = row % halves * ROWS, row // halves * LANES
            for line in range(lines):
                partial[step, row, line] = totals[line][top : top + ROWS, left : left + LANES]
        for index in range(1, owners):
            w = along(index)
            remote(
                partial.at[step, lax.div(w, blocks)],
                gathered.at[step, my_row],
                partial_sent.at[step, index],
                partial_sem.at[step],
                (w, mine),
            ).start()
        pltpu.make_async_copy(
            partial.at[step, my_row], gathered.at[step, my_row], partial_sem.at[step]
        ).start()
        wait_bytes(gathered.at[step], partial_sem.at[step])
        for line in range(lines):
            total = gathered[step, 0, line]
            for row in range(1, owners):
                total = total + gathered[step, row, line]
            sums[step, line] = total.astype(WIRE)

        here = utility.at[step, mine, :, my_rows, my_lanes]
        arrival = sums_sem.at[step, my_block]
        for index in range(1, owners):
            remote(
                sums.at[step], here, sums_sent.at[step, index], arrival, (along(index), mine)
            ).start()
        pltpu.make_async_copy(sums.at[step], here, arrival).start()
        update(step, mine, True)

    final = STEPS - 1
    outs = [
        pltpu.make_async_copy(
            state.at[player, my_levels], logits_out.at[player], out_sem.at[0, index]
        )
        for index, player in enumerate((mine, other))
    ] + [
        pltpu.make_async_copy(shown.at[player], utility_out.at[player], out_sem.at[1, index])
        for index, player in enumerate((mine, other))
    ]
    outs[0].start()
    outs[2].start()
    update(final, other, False)
    outs[1].start()
    outs[3].start()
    for copy in level_copies:
        copy.wait_send()
    pot_copy.wait_send()
    for core, count in enumerate((blocks, blocks - 1)):
        wait_bytes(parents.at[core, pl.ds(0, count)], parent_sent)
    for step in range(STEPS):
        for core, count in enumerate((blocks, blocks - 1)):
            wait_bytes(parts.at[step, core, pl.ds(0, count)], parts_sent.at[step])
        for index in range(1, owners):
            wait_bytes(partial.at[step, 0], partial_sent.at[step, index])
            wait_bytes(sums.at[step], sums_sent.at[step, index])
        for hop in range(1, blocks):
            wait_bytes(
                utility.at[step, mine, :, :, lanes_of(my_block)], sums_sent.at[step, owners + hop]
            )

        @pl.loop(0, blocks)
        def _(block):
            wait_bytes(utility.at[step, mine, :, :, lanes_of(block)], pass_sent.at[step, block])

    for out in outs:
        out.wait()


def solve(wide, plan_logits, pot_size, payoff_tiles, parent_first, parent_second):
    devices = wide * 2
    players, own_levels, lines, beliefs, buckets = plan_logits.shape
    levels = own_levels * 2
    whole = (players, levels, lines, beliefs, buckets)
    tile = (ROWS, LANES)
    blocks = buckets // next(width for width in (SPAN, LANES) if buckets % width == 0)
    owners = wide // blocks
    dma = pltpu.SemaphoreType.DMA
    return pl.pallas_call(
        functools.partial(solve_kernel, wide),
        out_shape=(
            jax.ShapeDtypeStruct(plan_logits.shape, jnp.float32),
            jax.ShapeDtypeStruct((players, lines, beliefs, buckets), jnp.float32),
        ),
        in_specs=[
            pl.BlockSpec(memory_space=pltpu.HBM),
            pl.BlockSpec(memory_space=pltpu.SMEM),
            pl.BlockSpec(memory_space=pltpu.HBM),
            pl.BlockSpec(memory_space=pltpu.SMEM),
            pl.BlockSpec(memory_space=pltpu.SMEM),
        ],
        out_specs=(
            pl.BlockSpec(memory_space=pl.ANY),
            pl.BlockSpec(memory_space=pl.ANY),
        ),
        scratch_shapes=[
            pltpu.VMEM(whole, jnp.float32),
            pltpu.VMEM(whole, jnp.float32),
            pltpu.VMEM((2, buckets, buckets), jnp.bfloat16),
            pltpu.VMEM((levels, lines, 8, LANES), jnp.float32),
            pltpu.VMEM((players, 1, LANES), jnp.int32),
            pltpu.VMEM((2, blocks, 1, LANES), jnp.int32),
            pltpu.VMEM((players, beliefs, buckets), jnp.bfloat16),
            pltpu.VMEM((players, levels, lines, beliefs, LANES), jnp.float32),
            pltpu.VMEM((players, levels, lines, beliefs, LANES), jnp.float32),
            pltpu.VMEM((STEPS, players, beliefs, buckets), WIRE),
            pltpu.VMEM((STEPS, 2, blocks, beliefs, buckets // blocks), WIRE),
            pltpu.VMEM((STEPS, owners, lines) + tile, jnp.float32),
            pltpu.VMEM((STEPS, owners, lines) + tile, jnp.float32),
            pltpu.VMEM((STEPS, lines) + tile, WIRE),
            pltpu.VMEM((STEPS, players, lines, beliefs, buckets), WIRE),
            pltpu.VMEM((players, lines, beliefs, buckets), jnp.float32),
            pltpu.VMEM((beliefs, buckets), jnp.float32),
            dma((2,)),
            dma((2,)),
            dma,
            dma,
            dma,
            dma,
            dma,
            dma((STEPS, 2)),
            dma((STEPS,)),
            dma((STEPS,)),
            dma((STEPS, owners)),
            dma((STEPS, blocks)),
            dma((STEPS, owners + blocks)),
            dma((STEPS, blocks)),
            dma((STEPS, blocks)),
            dma((2, 2)),
        ],
        compiler_params=pltpu.CompilerParams(
            collective_id=0, has_side_effects=True, vmem_limit_bytes=60 * 1024 * 1024
        ),
    )(plan_logits, pot_size, payoff_tiles, parent_first, parent_second)


def choose(wide, narrow, *arrays):
    players, _, _, beliefs, buckets = arrays[0].shape
    units = players * (beliefs // ROWS) * (buckets // LANES)
    whole_tiles = beliefs % ROWS == 0 and buckets % LANES == 0
    if whole_tiles and units == wide * narrow and arrays[2].shape[0] == 1 and narrow == 2:
        return solve(wide, *arrays)
    return per_device(*arrays)


def solution(mesh):
    in_specs = (
        P(None, "narrow", None, None, None),
        P("narrow", None),
        P(("wide", "narrow"), None, None),
        P(("wide", "narrow")),
        P(("wide", "narrow")),
    )
    out_specs = (P(None, "narrow", None, None, None), P())
    return jax.shard_map(
        functools.partial(choose, mesh.shape["wide"], mesh.shape["narrow"]),
        mesh=mesh,
        in_specs=in_specs,
        out_specs=out_specs,
        check_vma=False,
    )
```

```python
import functools

import jax
import jax.numpy as jnp
from jax import lax
from jax.experimental import pallas as pl
from jax.experimental.pallas import tpu as pltpu
from jax.sharding import PartitionSpec as P

STEPS = 3
ROWS = 16
LANES = 128
SPAN = 256
WIRE = jnp.bfloat16
SCALE = 1.0
MESH = pl.DeviceIdType.MESH


learning_rate = 1.0


def per_device(plan_logits, pot_size, payoff_tiles, parent_first, parent_second):
    logits = plan_logits
    line_count = logits.shape[2]
    level_index = lax.axis_index("narrow")
    line_ids = jnp.arange(line_count, dtype=jnp.int32)[None, :]
    pick_first = (parent_first[:, None] == line_ids).astype(jnp.bfloat16)
    pick_second = (parent_second[:, None] == line_ids).astype(jnp.bfloat16)
    sum_first = pick_first.astype(jnp.float32)
    sum_second = pick_second.astype(jnp.float32)
    previous = None
    utility = None
    for iteration in range(STEPS):
        keep = jax.nn.log_sigmoid(logits)
        local_keep = None
        local_fold = None
        every_logit, every_pot = (
            lax.all_gather(logits, "narrow", axis=1, tiled=True),
            lax.all_gather(pot_size, "narrow", axis=0, tiled=True),
        )
        every_keep = jax.nn.log_sigmoid(every_logit)
        every_prefix = jnp.cumsum(every_keep, axis=1) - every_keep
        reached = jnp.exp(jnp.sum(every_keep, axis=1)).astype(jnp.bfloat16)
        every_mass = jnp.mean(jnp.exp(every_prefix), axis=4)[::-1]
        every_fold = (-every_pot[None, :, :, None] * every_mass)[..., None]
        every_log_fold = jax.nn.log_sigmoid(-every_logit) + learning_rate * every_fold
        fold_value = lax.dynamic_slice_in_dim(every_fold, level_index, 1, 1)
        level_count = every_keep.shape[1]
        acc_keep = jnp.zeros_like(keep[:, 0])
        acc_fold = jnp.full_like(keep[:, 0], -jnp.inf)
        local_keep = jnp.zeros_like(keep[:, 0])
        local_fold = jnp.zeros_like(keep[:, 0])
        for level in range(level_count - 1, -1, -1):
            mine = level_index == level
            local_keep = jnp.where(mine, acc_keep, local_keep)
            local_fold = jnp.where(mine, acc_fold, local_fold)
            acc_fold = jnp.logaddexp(every_keep[:, level] + acc_fold, every_log_fold[:, level])
            acc_keep = every_keep[:, level] + acc_keep
        local_keep = local_keep[:, None]
        local_fold = local_fold[:, None]
        first_reach = jnp.einsum(
            "ls,sbj->lbj", pick_first, reached[0], preferred_element_type=jnp.float32
        ).astype(jnp.bfloat16)
        second_reach = jnp.einsum(
            "ls,sbj->lbj", pick_second, reached[1], preferred_element_type=jnp.float32
        ).astype(jnp.bfloat16)
        value_first = jnp.einsum(
            "lbj,lij->lbi", second_reach, payoff_tiles, preferred_element_type=jnp.float32
        )
        value_second = -jnp.einsum(
            "lbi,lij->lbj", first_reach, payoff_tiles, preferred_element_type=jnp.float32
        )
        local_sums = jnp.stack(
            [
                jnp.einsum("ls,lbi->sbi", sum_first, value_first, precision=lax.Precision.HIGHEST),
                jnp.einsum(
                    "ls,lbi->sbi", sum_second, value_second, precision=lax.Precision.HIGHEST
                ),
            ]
        )
        suffix_keep, suffix_fold = (local_keep, local_fold)
        utility = lax.psum(local_sums, ("wide", "narrow"))
        if previous is None:
            previous = utility
        target = 2.0 * utility - previous
        previous = utility
        next_value = (
            jnp.logaddexp(suffix_keep + learning_rate * target[:, None], suffix_fold)
            / learning_rate
        )
        logits = logits + learning_rate * (next_value - fold_value)
    return (logits, utility)


def softplus(x):
    return jnp.maximum(x, 0.0) + jnp.log(1.0 + jnp.exp(-jnp.abs(x)))


def wait_bytes(ref, sem):
    pltpu.make_async_copy(ref, ref, sem).wait()


def solve_kernel(
    wide,
    logits_ref,
    pot_ref,
    payoff_ref,
    first_ref,
    second_ref,
    logits_out,
    utility_out,
    state,
    soft,
    payoff,
    pots,
    parent,
    parents,
    reach,
    mass,
    fold,
    values,
    parts,
    sums,
    utility,
    shown,
    level_sem,
    level_sent,
    pot_sem,
    pot_sent,
    parent_sem,
    parent_sent,
    payoff_sem,
    parts_sem,
    parts_sent,
    sums_sem,
    sums_sent,
    pass_sem,
    pass_sent,
    out_sem,
):
    narrow = 2
    devices = wide * narrow
    _, levels, lines, beliefs, buckets = state.shape
    own_levels = logits_ref.shape[1]
    halves = beliefs // ROWS
    my_wide, mine = lax.axis_index("wide"), lax.axis_index("narrow")
    other = 1 - mine
    me = my_wide * narrow + mine
    my_levels = pl.ds(mine * own_levels, own_levels)
    span = next(width for width in (SPAN, LANES) if buckets % width == 0)

    def remote(src, dst, sent, received, device):
        return pltpu.make_async_remote_copy(
            src_ref=src,
            dst_ref=dst,
            send_sem=sent,
            recv_sem=received,
            device_id=device,
            device_id_type=MESH,
        )

    def place(tile):
        half = lax.rem(tile, halves)
        chunk = lax.div(tile, halves)
        return (
            pl.ds(pl.multiple_of(half * ROWS, ROWS), ROWS),
            pl.ds(pl.multiple_of(chunk * LANES, LANES), LANES),
        )

    my_rows, my_lanes = place(my_wide)

    load = pltpu.make_async_copy(payoff_ref.at[0], payoff.at[0], payoff_sem)
    load.start()
    pltpu.make_async_copy(logits_ref, state.at[:, my_levels], level_sem).start()

    barrier = pltpu.get_barrier_semaphore()

    @pl.loop(1, devices)
    def _(step):
        device = lax.rem(me + step, devices)
        pl.semaphore_signal(
            barrier,
            inc=1,
            device_id=(lax.div(device, narrow), lax.rem(device, narrow)),
            device_id_type=MESH,
        )

    parent[0] = jnp.full((1, LANES), first_ref[0], jnp.int32)
    parent[1] = jnp.full((1, LANES), second_ref[0], jnp.int32)
    for level in range(own_levels):
        for line in range(lines):
            pots[mine * own_levels + level, line] = jnp.full(
                (8, LANES), pot_ref[level, line], jnp.float32
            )
    mass[...] = jnp.zeros_like(mass)
    pl.semaphore_wait(barrier, devices - 1)

    sibling = (my_wide, other)
    level_copy = remote(logits_ref, state.at[:, my_levels], level_sent, level_sem, sibling)
    level_copy.start()
    pot_copy = remote(pots.at[my_levels], pots.at[my_levels], pot_sent, pot_sem, sibling)
    pot_copy.start()

    @pl.loop(0, wide)
    def _(step):
        w = lax.rem(my_wide + step, wide)
        remote(parent.at[other], parents.at[me], parent_sent, parent_sem, (w, other)).start()

    @pl.loop(1, wide)
    def _(step):
        w = lax.rem(my_wide + step, wide)
        remote(parent.at[mine], parents.at[me], parent_sent, parent_sem, (w, mine)).start()

    pltpu.make_async_copy(parent.at[mine], parents.at[me], parent_sem).start()

    load.wait()
    side = min(256, buckets)
    for row in range(0, buckets, side):
        for column in range(0, buckets, side):
            payoff[1, column : column + side, row : row + side] = payoff[
                0, row : row + side, column : column + side
            ].T
    wait_bytes(pots.at[pl.ds(0, levels - own_levels)], pot_sem)
    wait_bytes(state, level_sem)

    def finish_block(player, lanes, fresh):
        chosen = None
        for line in range(lines):
            total = None
            for level in range(levels):
                logit, plus = fresh[line][level]
                if level:
                    lost = jnp.exp(total)
                    part = lost[:, :LANES]
                    for column in range(LANES, span, LANES):
                        part = part + lost[:, column : column + LANES]
                    mass[player, level, line] += part
                total = logit - plus if total is None else total + (logit - plus)
            if chosen is None:
                chosen = total
            else:
                picked = jnp.broadcast_to(parent[player][:, :1], (beliefs, span)) == line
                chosen = jnp.where(picked, total, chosen)
        reach[player, :, lanes] = jnp.exp(chosen).astype(jnp.bfloat16)

    def finish_fold():
        for player in range(2):
            for line in range(lines):
                for level in range(levels):
                    pot = pots[level, line, 0:1, :]
                    if level:
                        mean = jnp.sum(
                            mass[1 - player, level, line], axis=-1, keepdims=True
                        ) * (1.0 / buckets)
                        fold[player, level, line] = -(pot * mean)
                    else:
                        fold[player, level, line] = jnp.broadcast_to(-pot, (beliefs, LANES))

    def begin(player):
        @pl.loop(0, buckets // span)
        def _(block):
            lanes = pl.ds(pl.multiple_of(block * span, span), span)
            fresh = []
            for line in range(lines):
                of_line = []
                for level in range(levels):
                    logit = state[player, level, line, :, lanes]
                    of_line.append((logit, softplus(logit)))
                fresh.append(of_line)
            for line in range(lines):
                for level in range(levels):
                    soft[player, level, line, :, lanes] = fresh[line][level][1]
            finish_block(player, lanes, fresh)

    def update(step, player):
        last = step == STEPS - 1

        @pl.loop(0, buckets // span)
        def _(block):
            lanes = pl.ds(pl.multiple_of(block * span, span), span)
            old, seen, lost = {}, {}, {}
            for line in range(lines):
                now = utility[step, player, line, :, lanes].astype(jnp.float32) * (1.0 / SCALE)
                seen[line] = now, now
                if step:
                    before = utility[step - 1, player, line, :, lanes].astype(jnp.float32)
                    seen[line] = now, 2.0 * now - before * (1.0 / SCALE)
                for level in range(levels):
                    here = (player, level, line, slice(None), lanes)
                    old[line, level] = state[here], soft[here]
                    lost[line, level] = jnp.concatenate(
                        [fold[player, level, line]] * (span // LANES), axis=1
                    )
            fresh = []
            for line in range(lines):
                value = seen[line][1]
                of_line = [None] * levels
                for level in range(levels - 1, -1, -1):
                    logit = old[line, level][0] + (value - lost[line, level])
                    plus = None
                    if level or not last:
                        plus = softplus(logit)
                        value = lost[line, level] + (plus - old[line, level][1])
                    of_line[level] = logit, plus
                fresh.append(of_line)
            for line in range(lines):
                for level in range(levels):
                    here = (player, level, line, slice(None), lanes)
                    state[here] = fresh[line][level][0]
                    if not last:
                        soft[here] = fresh[line][level][1]
                if last:
                    shown[player, line, :, lanes] = seen[line][0]
            if not last:
                finish_block(player, lanes, fresh)

    def respond(step, player):
        target = 1 - player
        factor = jnp.where(player == 0, -SCALE, SCALE).astype(jnp.float32)
        for start in range(0, buckets, side):
            product = jnp.dot(
                reach[player],
                payoff[player, :, start : start + side],
                preferred_element_type=jnp.float32,
            )
            values[step, target, :, start : start + side] = (product * factor).astype(WIRE)

    def send_part(step, target, w):
        rows, lanes = place(w)
        return (
            values.at[step, target, rows, lanes],
            parts.at[step, me],
            parts_sent.at[step],
            parts_sem.at[step],
            (w, target),
        )

    begin(mine)
    for step in range(STEPS):
        respond(step, mine)

        @pl.loop(0, wide)
        def _(index):
            w = lax.rem(my_wide + index, wide)
            remote(*send_part(step, other, w)).start()

        if step:
            wait_bytes(utility.at[step - 1, other], pass_sem.at[step - 1])
            update(step - 1, other)
        else:
            begin(other)
        respond(step, other)

        @pl.loop(1, wide)
        def _(index):
            w = lax.rem(my_wide + index, wide)
            remote(*send_part(step, mine, w)).start()

        own = values.at[step, mine, my_rows, my_lanes]
        pltpu.make_async_copy(own, parts.at[step, me], parts_sem.at[step]).start()
        finish_fold()
        mass[...] = jnp.zeros_like(mass)
        if step == 0:
            wait_bytes(parents, parent_sem)
        wait_bytes(parts.at[step], parts_sem.at[step])

        def add(device, totals):
            part = parts[step, device].astype(jnp.float32)
            owner = jnp.broadcast_to(parents[device], (ROWS, LANES))
            return tuple(
                total + jnp.where(owner == line, part, 0.0) for line, total in enumerate(totals)
            )

        zero = jnp.zeros((ROWS, LANES), jnp.float32)
        totals = lax.fori_loop(0, devices, add, (zero,) * lines, unroll=8)
        for line in range(lines):
            sums[step, line] = totals[line].astype(WIRE)

        here = utility.at[step, mine, :, my_rows, my_lanes]

        @pl.loop(1, wide)
        def _(index):
            w = lax.rem(my_wide + index, wide)
            remote(
                sums.at[step], here, sums_sent.at[step, index], sums_sem.at[step], (w, mine)
            ).start()

        pltpu.make_async_copy(sums.at[step], here, sums_sem.at[step]).start()
        half = utility.at[step, mine]
        wait_bytes(half, sums_sem.at[step])
        remote(half, half, pass_sent.at[step], pass_sem.at[step], sibling).start()
        update(step, mine)

    final = STEPS - 1
    outs = [
        pltpu.make_async_copy(
            state.at[player, my_levels], logits_out.at[player], out_sem.at[0, index]
        )
        for index, player in enumerate((mine, other))
    ] + [
        pltpu.make_async_copy(shown.at[player], utility_out.at[player], out_sem.at[1, index])
        for index, player in enumerate((mine, other))
    ]
    outs[0].start()
    outs[2].start()
    wait_bytes(utility.at[final, other], pass_sem.at[final])
    update(final, other)
    outs[1].start()
    outs[3].start()
    level_copy.wait_send()
    pot_copy.wait_send()
    wait_bytes(parents.at[pl.ds(0, devices - 1)], parent_sent)
    for step in range(STEPS):
        wait_bytes(parts.at[step, pl.ds(0, devices - 1)], parts_sent.at[step])
        wait_bytes(utility.at[step, mine], pass_sent.at[step])

        @pl.loop(1, wide)
        def _(index):
            wait_bytes(sums.at[step], sums_sent.at[step, index])

    for out in outs:
        out.wait()


def solve(wide, plan_logits, pot_size, payoff_tiles, parent_first, parent_second):
    devices = wide * 2
    players, own_levels, lines, beliefs, buckets = plan_logits.shape
    levels = own_levels * 2
    whole = (players, levels, lines, beliefs, buckets)
    tile = (ROWS, LANES)
    dma = pltpu.SemaphoreType.DMA
    return pl.pallas_call(
        functools.partial(solve_kernel, wide),
        out_shape=(
            jax.ShapeDtypeStruct(plan_logits.shape, jnp.float32),
            jax.ShapeDtypeStruct((players, lines, beliefs, buckets), jnp.float32),
        ),
        in_specs=[
            pl.BlockSpec(memory_space=pltpu.HBM),
            pl.BlockSpec(memory_space=pltpu.SMEM),
            pl.BlockSpec(memory_space=pltpu.HBM),
            pl.BlockSpec(memory_space=pltpu.SMEM),
            pl.BlockSpec(memory_space=pltpu.SMEM),
        ],
        out_specs=(
            pl.BlockSpec(memory_space=pl.ANY),
            pl.BlockSpec(memory_space=pl.ANY),
        ),
        scratch_shapes=[
            pltpu.VMEM(whole, jnp.float32),
            pltpu.VMEM(whole, jnp.float32),
            pltpu.VMEM((2, buckets, buckets), jnp.bfloat16),
            pltpu.VMEM((levels, lines, 8, LANES), jnp.float32),
            pltpu.VMEM((players, 1, LANES), jnp.int32),
            pltpu.VMEM((devices, 1, LANES), jnp.int32),
            pltpu.VMEM((players, beliefs, buckets), jnp.bfloat16),
            pltpu.VMEM((players, levels, lines, beliefs, LANES), jnp.float32),
            pltpu.VMEM((players, levels, lines, beliefs, LANES), jnp.float32),
            pltpu.VMEM((STEPS, players, beliefs, buckets), WIRE),
            pltpu.VMEM((STEPS, devices) + tile, WIRE),
            pltpu.VMEM((STEPS, lines) + tile, WIRE),
            pltpu.VMEM((STEPS, players, lines, beliefs, buckets), WIRE),
            pltpu.VMEM((players, lines, beliefs, buckets), jnp.float32),
            dma,
            dma,
            dma,
            dma,
            dma,
            dma,
            dma,
            dma((STEPS,)),
            dma((STEPS,)),
            dma((STEPS,)),
            dma((STEPS, wide)),
            dma((STEPS,)),
            dma((STEPS,)),
            dma((2, 2)),
        ],
        compiler_params=pltpu.CompilerParams(
            collective_id=0, has_side_effects=True, vmem_limit_bytes=52 * 1024 * 1024
        ),
    )(plan_logits, pot_size, payoff_tiles, parent_first, parent_second)


def choose(wide, narrow, *arrays):
    players, _, _, beliefs, buckets = arrays[0].shape
    units = players * (beliefs // ROWS) * (buckets // LANES)
    whole_tiles = beliefs % ROWS == 0 and buckets % LANES == 0
    if whole_tiles and units == wide * narrow and arrays[2].shape[0] == 1 and narrow == 2:
        return solve(wide, *arrays)
    return per_device(*arrays)


def solution(mesh):
    in_specs = (
        P(None, "narrow", None, None, None),
        P("narrow", None),
        P(("wide", "narrow"), None, None),
        P(("wide", "narrow")),
        P(("wide", "narrow")),
    )
    out_specs = (P(None, "narrow", None, None, None), P())
    return jax.shard_map(
        functools.partial(choose, mesh.shape["wide"], mesh.shape["narrow"]),
        mesh=mesh,
        in_specs=in_specs,
        out_specs=out_specs,
        check_vma=False,
    )
```
